256 devices in a mesh: ctx: 32 (over y, z_lo, x), tp: 8 (over z_hi, core).
Axes of the slice: x: 4, y: 4, z: 8 (z_hi: 4, z_lo: 2; z = z_hi * 2 + z_lo), core: 2. Of those that a mesh axis runs over, the one named last changes fastest.
Arguments:
- stream_first: bfloat16 [4096, 3072], P('ctx', 'tp'), may hold values from -6 to 6
- stream_second: bfloat16 [4096, 3072], P('ctx', 'tp'), may hold values from -6 to 6
- grad_first: bfloat16 [4096, 3072], P('ctx', 'tp'), may hold values from -6 to 6
- grad_second: bfloat16 [4096, 3072], P('ctx', 'tp'), may hold values from -6 to 6
- expert_ids: int32 [4096, 4], P('ctx'), may hold values from 0 to 31, all different within a row; in each aligned block of 128 rows (0 to 127, 128 to 255, ...) at most 32 rows name the same one
- gate_probs: float32 [4096, 4], P('ctx'), may hold values from 0.05 to 1
- w_in: bfloat16 [32, 3072, 2048], P('ctx', None, 'tp'), may hold values from -0.109375 to 0.109375
- w_out: bfloat16 [32, 2048, 3072], P('ctx', 'tp'), may hold values from -0.125 to 0.125
Outputs:
- stream_input: bfloat16 [4096, 3072], P('ctx', 'tp')
- grad_stream: bfloat16 [4096, 3072], P('ctx', 'tp')
- grad_w_in: float32 [32, 3072, 2048], P('ctx', None, 'tp')
- grad_w_out: float32 [32, 2048, 3072], P('ctx', 'tp')
- grad_gates: float32 [4096, 4], P('ctx')
The draws below stay inside these ranges and needn't reach their ends.
Inputs may be any that keep to these rules, and one draw needn't show every extreme that they name: `expert_ids`: each row names 4 different experts. In each aligned block of 128 rows (the rows of one index of ctx) no expert is named more than 32 times, a bound that some block reaches.
All inputs are finite; a program needn't handle non-finite values.
Results may differ from the reference program's by a relative error of at most 0.017.
Values may be sent and summed in bfloat16 or wider, within the bound.
No kernel may reach another device: no remote copies, remote signals or barrier semaphores. Data moves between devices by JAX's collectives and lax.ppermute only.
A program may use at most 192 MiB of HBM per device.

```python
import math
import jax
import jax.numpy as jnp
import numpy as np
from jax import lax

D = 3072
FF = 2048
TOPK = 4
TOK_DEV = 128
EXPERTS = 32
TOKENS = 4096
CAP = 32
N_TP = 8


def shard_levels(own_key, shape, pieces, least, top_value):
    def one(dim, shards_of):
        steps = jax.random.uniform(jax.random.fold_in(jax.random.fold_in(own_key, 6), dim), (shards_of,), jnp.float32, least / len(pieces), top_value / len(pieces))
        return jnp.repeat(jnp.exp(steps), shape[dim] // shards_of).reshape((-1,) + (1,) * (len(shape) - dim - 1))

    loudness = one(*pieces[0])
    for cut in pieces[1:]:
        loudness = loudness * one(*cut)
    return loudness


def routed_block(key, own, number, rows, amount, top, reach, slope):
    sequence = jax.random.permutation(key, amount)
    heavy_load, usual = load_shares(amount, rows * top, reach, slope, True), load_shares(amount, rows * top, reach, slope, False)
    places = jnp.arange(amount)

    def named(tallies, offset_by):
        used = int((tallies > 0).sum())
        fixed = max(1, used // 4)
        moved = fixed + (places - fixed + offset_by * (used - fixed)) % max(1, amount - fixed)
        return jnp.zeros((amount,), jnp.int32).at[sequence[jnp.where(places < fixed, places, moved)]].set(jnp.asarray(tallies, jnp.int32))

    tallies = jnp.where(number % 4 == 0, named(heavy_load, number // 4), named(usual, number - number // 4 - 1))
    mixed = jax.random.permutation(jax.random.fold_in(own, 3), amount)
    source_of, sink = mixed[0:amount // 2 * 2:2], mixed[1:amount // 2 * 2:2]
    room = jnp.minimum(tallies[source_of] - 1, reach - tallies[sink]) // 2
    room = jnp.where((source_of == sequence[0]) | (sink == sequence[0]) | (tallies[sink] == 0), 0, jnp.maximum(room, 0))
    moved = jax.random.randint(jax.random.fold_in(own, 4), (amount // 2,), 0, 1 << 20) % (room + 1)
    tallies = tallies.at[source_of].add(-moved).at[sink].add(moved)
    items = jnp.searchsorted(jnp.cumsum(tallies), jnp.arange(rows * top), side="right").astype(jnp.int32)
    listing = items.reshape(top, rows).T
    listing = listing[jax.random.permutation(jax.random.fold_in(own, 1), rows)]
    offset_by = jax.random.randint(jax.random.fold_in(own, 2), (rows, 1), 0, top)
    return jnp.take_along_axis(listing, (jnp.arange(top)[None, :] + offset_by) % top, axis=1)


def load_shares(number_of, total, bound, lean, full):
    weights = [(1 << 20) // math.isqrt(grade ** lean) + 1 for grade in range(1, number_of + 1)]
    largest = bound if full else min(bound, max(-(-total // number_of), total * weights[0] // sum(weights)))
    least = 1 if total - largest >= number_of - 1 else 0
    holding, rest = [largest] + [least] * (number_of - 1), total - largest - least * (number_of - 1)
    while rest > 0:
        candidates = [i for i in range(1, number_of) if holding[i] < largest] or [i for i in range(1, number_of) if holding[i] < bound]
        mass, budget = sum([weights[i] for i in candidates]), rest
        for i in candidates:
            more = min(bound - holding[i], max(1, budget * weights[i] // mass), rest)
            holding[i] = holding[i] + more
            rest = rest - more
    return np.array(holding)


def bell_draw(own_key, shape, width, limit, shards=(), kind=jnp.bfloat16):
    values = jax.random.normal(own_key, shape, jnp.float32) * width
    if len(shards) > 0:
        values = shard_levels(own_key, shape, shards, -0.22, 0.18) * values
    return jnp.clip(values, min=-limit, max=limit).astype(kind)


def setup_inputs(seed: int = 0) -> dict:
    key_list = jax.random.split(jax.random.key(seed), 9)
    stream_first = bell_draw(key_list[0], (TOKENS, D), 1.0, 6.0, ((0, 32), (1, 8)))
    stream_second = bell_draw(key_list[1], (TOKENS, D), 0.5, 6.0, ((0, 32), (1, 8)))
    grad_first = bell_draw(key_list[2], (TOKENS, D), 0.5, 6.0, ((0, 32), (1, 8)))
    grad_second = bell_draw(key_list[3], (TOKENS, D), 1.0, 6.0, ((0, 32), (1, 8)))
    expert_ids_keys = jax.random.split(jax.random.fold_in(key_list[4], 1), TOKENS // TOK_DEV)
    expert_ids_turns = jax.random.permutation(jax.random.fold_in(key_list[4], 3), TOKENS // TOK_DEV)
    expert_ids = jax.vmap(lambda own, number: routed_block(jax.random.fold_in(key_list[4], 2), own, number, TOK_DEV, EXPERTS, TOPK, CAP, 2))(expert_ids_keys, expert_ids_turns).reshape((TOKENS, TOPK))
    gate_probs = jnp.clip(jnp.exp(math.log(1.0) - 2.9957323 * jax.random.uniform(key_list[5], (TOKENS, TOPK), jnp.float32) ** shard_levels(key_list[5], (TOKENS, TOPK), ((0, 32),), -0.2, 0.2)), 0.05, 1.0)
    w_in = bell_draw(key_list[6], (EXPERTS, D, FF), D ** -0.5, 0.109375, ((0, 32), (2, 8)))
    w_out = bell_draw(key_list[7], (EXPERTS, FF, D), FF ** -0.5, 0.125, ((0, 32), (1, 8)))
    return dict(stream_first=stream_first, stream_second=stream_second, grad_first=grad_first, grad_second=grad_second, expert_ids=expert_ids, gate_probs=gate_probs, w_in=w_in, w_out=w_out)


def gelu_value(x):
    return x * 0.5 * (1.0 + lax.erf(x * 0.7071067811865476))

def gelu_slope(x):
    return 0.5 * (1.0 + lax.erf(x * 0.7071067811865476)) + x * jnp.exp(-0.5 * x * x) * 0.3989422804014327

def reference(stream_first, stream_second, grad_first, grad_second, expert_ids, gate_probs, w_in, w_out):
    first = stream_first.astype(jnp.float32)
    mean = lax.optimization_barrier(jnp.mean(first, axis=1, keepdims=True))
    centred = first - mean
    rstd = lax.rsqrt(lax.optimization_barrier(jnp.mean(centred * centred, axis=1, keepdims=True)) + 1e-05)
    normed = centred * rstd
    normed_low = normed.astype(jnp.bfloat16)
    routes = TOKENS * TOPK
    blocks = TOKENS // TOK_DEV
    flat = expert_ids.reshape(blocks, TOK_DEV * TOPK)
    onehot = (flat[:, :, None] == jnp.arange(EXPERTS, dtype=jnp.int32)[None, None, :]).astype(jnp.int32)
    rank = lax.optimization_barrier(jnp.sum(jnp.cumsum(onehot, axis=1) * onehot, axis=2)) - 1
    column = jnp.arange(blocks, dtype=jnp.int32)[:, None] * CAP + rank
    route_at = jnp.full((EXPERTS, blocks * CAP), routes, jnp.int32)
    route_at = route_at.at[flat.reshape(routes), column.reshape(routes)].set(jnp.arange(routes, dtype=jnp.int32))
    gate_flat = gate_probs.reshape(routes)
    dy_second = grad_second.astype(jnp.float32)
    scaled = (gate_probs[:, :, None] * dy_second[:, None, :]).astype(jnp.bfloat16).reshape(routes, D)
    group = FF // N_TP

    def one_expert(carry, inputs):
        branch, grad_normed, gate_grad = carry
        weight_in, weight_out, slots = inputs
        valid = slots < routes
        safe = jnp.minimum(slots, routes - 1)
        token = safe // TOPK
        rows = jnp.where(valid[:, None], normed_low[token], jnp.zeros((), jnp.bfloat16))
        grad_rows = jnp.where(valid[:, None], scaled[safe], jnp.zeros((), jnp.bfloat16))
        preact = jnp.dot(rows, weight_in, preferred_element_type=jnp.float32)
        hidden = gelu_value(preact).astype(jnp.bfloat16)
        parts = jnp.einsum('skf,kfd->ksd', hidden.astype(jnp.float32).reshape(-1, N_TP, group), weight_out.astype(jnp.float32).reshape(N_TP, group, D))
        result = lax.optimization_barrier(jnp.sum(lax.optimization_barrier(parts.astype(jnp.bfloat16)).astype(jnp.float32), axis=0))
        grad_hidden = lax.dot_general(grad_rows, weight_out, (((1,), (1,)), ((), ())), preferred_element_type=jnp.float32)
        grad_pre = (grad_hidden * gelu_slope(preact)).astype(jnp.bfloat16)
        grad_out_e = lax.dot_general(hidden, grad_rows, (((0,), (0,)), ((), ())), preferred_element_type=jnp.float32)
        grad_in_e = lax.dot_general(rows, grad_pre, (((0,), (0,)), ((), ())), preferred_element_type=jnp.float32)
        dparts = jnp.einsum('skf,dkf->ksd', grad_pre.astype(jnp.float32).reshape(-1, N_TP, group), weight_in.astype(jnp.float32).reshape(D, N_TP, group))
        route_dx = lax.optimization_barrier(jnp.sum(lax.optimization_barrier(dparts.astype(jnp.bfloat16)).astype(jnp.float32), axis=0))
        token_drop = jnp.where(valid, token, TOKENS)
        route_drop = jnp.where(valid, safe, routes)
        weight = jnp.where(valid, gate_flat[safe], 0.0)
        branch = branch.at[token_drop].add(weight[:, None] * result, mode='drop')
        grad_normed = grad_normed.at[token_drop].add(route_dx, mode='drop')
        inner = lax.optimization_barrier(jnp.sum(dy_second[token] * result, axis=1))
        gate_grad = gate_grad.at[route_drop].set(inner, mode='drop')
        return ((branch, grad_normed, gate_grad), (grad_in_e, grad_out_e))
    start = (jnp.zeros((TOKENS, D), jnp.float32), jnp.zeros((TOKENS, D), jnp.float32), jnp.zeros((routes,), jnp.float32))
    (branch, grad_normed, gate_grad), (grad_w_in, grad_w_out) = lax.scan(one_expert, start, (w_in, w_out, route_at))
    stream_input = (stream_second.astype(jnp.float32) - branch).astype(jnp.bfloat16)
    mean_grad = lax.optimization_barrier(jnp.mean(grad_normed, axis=1, keepdims=True))
    mean_mixed = lax.optimization_barrier(jnp.mean(grad_normed * normed, axis=1, keepdims=True))
    grad_stream = (grad_first.astype(jnp.float32) + rstd * (grad_normed - mean_grad - normed * mean_mixed)).astype(jnp.bfloat16)
    return (stream_input, grad_stream, grad_w_in, grad_w_out, gate_grad.reshape(TOKENS, TOPK))
```

```python
import functools

import jax
import jax.numpy as jnp
from jax import lax
from jax.experimental import pallas as pl
from jax.experimental.pallas import tpu as pltpu
from jax.sharding import Mesh, PartitionSpec as P

F32 = jnp.float32
BF16 = jnp.bfloat16
CTX = ("y", "zl", "x")
CORES = ((0, 1), (1, 0))


def gelu_value(x):
    return x * 0.5 * (1.0 + lax.erf(x * 0.7071067811865476))


def gelu_slope(x):
    return (
        0.5 * (1.0 + lax.erf(x * 0.7071067811865476))
        + x * jnp.exp(-0.5 * x * x) * 0.3989422804014327
    )


def swap_cores(v):
    return lax.ppermute(v, "core", CORES)


def swap_chips(v, r):
    return lax.ppermute(v, "zh", [(i, i ^ r) for i in range(4)])


def gather_features(v):
    mine = [v] + [swap_chips(v, r) for r in (1, 2, 3)]
    return mine + [swap_cores(m) for m in mine]


def select_rows(qt, slots):
    topk, tokens = qt.shape
    at = lax.broadcasted_iota(jnp.int32, (slots, tokens), 0)
    hit = at == qt[0:1, :]
    for k in range(1, topk):
        hit = jnp.logical_or(hit, at == qt[k : k + 1, :])
    return hit


def pack_first_kernel(order, qt_ref, *refs):
    parts, (out_ref, full_ref, stats_ref, low, pick) = refs[:8], refs[8:]
    step = pl.program_id(0)

    @pl.when(step == 0)
    def _():
        width = 8 * parts[0].shape[1]
        total = sum(jnp.sum(p[...].astype(F32), axis=1, keepdims=True) for p in parts)
        mean = total / width
        square = sum(
            jnp.sum(jnp.square(p[...].astype(F32) - mean), axis=1, keepdims=True) for p in parts
        )
        rstd = lax.rsqrt(square / width + 1e-05)
        for i, p in enumerate(parts):
            low[i] = ((p[...].astype(F32) - mean) * rstd).astype(BF16)
        lane = lax.broadcasted_iota(jnp.int32, stats_ref.shape, 1)
        stats_ref[...] = jnp.where(lane == 0, mean, rstd)
        pick[...] = jnp.where(select_rows(qt_ref[...], pick.shape[0]), 1.0, 0.0).astype(BF16)

    for i, p in enumerate(parts):

        @pl.when(step == i)
        def _(p=p):
            full_ref[...] = p[...]

    out_ref[...] = jnp.dot(pick[...], low[step], preferred_element_type=F32).astype(BF16)


def pack_grad_kernel(order, qt_ref, gt_ref, *refs):
    parts, (out_ref, full_ref, pick, gate) = refs[:8], refs[8:]
    step = pl.program_id(0)

    @pl.when(step == 0)
    def _():
        slots = pick.shape[0]
        qt, gt = qt_ref[...], gt_ref[...]
        pick[...] = jnp.where(select_rows(qt, slots), 1.0, 0.0).astype(BF16)
        at = lax.broadcasted_iota(jnp.int32, (slots, qt.shape[1]), 0)
        weight = jnp.zeros((slots, qt.shape[1]), F32)
        for k in range(qt.shape[0]):
            weight = weight + jnp.where(at == qt[k : k + 1, :], gt[k : k + 1, :], 0.0)
        gate[...] = jnp.sum(weight, axis=1, keepdims=True)

    for i, p in enumerate(parts):

        @pl.when(step == i)
        def _(p=p):
            full_ref[...] = p[...]
            rows = jnp.dot(pick[...], p[...], preferred_element_type=F32)
            out_ref[...] = (gate[...] * rows).astype(BF16)


def store_parts(step, value, keep_ref, give_ref):
    @pl.when(step < 4)
    def _():
        keep_ref[0] = value.astype(BF16)

    @pl.when(step >= 4)
    def _():
        give_ref[0] = value.astype(BF16)


def combine_out_kernel(order, q_ref, g_ref, rows_ref, full_ref, keep_ref, give_ref, inner_ref, high, rest, inner):
    step = pl.program_id(0)

    @pl.when(step == 0)
    def _():
        lane = lax.broadcasted_iota(jnp.int32, inner.shape, 1)
        weight = jnp.zeros(inner.shape, F32)
        for k in range(q_ref.shape[1]):
            weight = weight + jnp.where(lane == q_ref[:, k : k + 1], g_ref[:, k : k + 1], 0.0)
        top = weight.astype(BF16)
        high[...] = top
        rest[...] = (weight - top.astype(F32)).astype(BF16)
        inner[...] = jnp.zeros_like(inner)

    rows = rows_ref[...]
    value = jnp.dot(high[...], rows, preferred_element_type=F32) + jnp.dot(
        rest[...], rows, preferred_element_type=F32
    )
    store_parts(step, value, keep_ref, give_ref)
    inner[...] += lax.dot_general(
        full_ref[...], rows, (((1,), (1,)), ((), ())), preferred_element_type=F32
    )

    @pl.when(step == 7)
    def _():
        lane = lax.broadcasted_iota(jnp.int32, inner.shape, 1)
        place = lax.broadcasted_iota(jnp.int32, inner_ref.shape, 1)
        found = jnp.zeros(inner_ref.shape, F32)
        for k in range(q_ref.shape[1]):
            one = jnp.sum(
                jnp.where(lane == q_ref[:, k : k + 1], inner[...], 0.0), axis=1, keepdims=True
            )
            found = found + jnp.where(place == k, one, 0.0)
        inner_ref[...] = found


def combine_dx_kernel(order, q_ref, inner_ref, stats_ref, rows_ref, full_ref, keep_ref, give_ref, sums_ref, pick, sums):
    step = pl.program_id(0)

    @pl.when(step == 0)
    def _():
        lane = lax.broadcasted_iota(jnp.int32, pick.shape, 1)
        hit = lane == q_ref[:, 0:1]
        for k in range(1, q_ref.shape[1]):
            hit = jnp.logical_or(hit, lane == q_ref[:, k : k + 1])
        pick[...] = jnp.where(hit, 1.0, 0.0).astype(BF16)
        sums[...] = jnp.zeros_like(sums)

    value = jnp.dot(pick[...], rows_ref[...], preferred_element_type=F32)
    store_parts(step, value, keep_ref, give_ref)
    normed = (full_ref[...].astype(F32) - stats_ref[:, 0:1]) * stats_ref[:, 1:2]
    place = lax.broadcasted_iota(jnp.int32, sums.shape, 1)
    plain = jnp.sum(value, axis=1, keepdims=True)
    mixed = jnp.sum(value * normed, axis=1, keepdims=True)
    sums[...] += jnp.where(place == 4, plain, 0.0) + jnp.where(place == 5, mixed, 0.0)

    @pl.when(step == 7)
    def _():
        sums_ref[...] = sums[...] + inner_ref[...]


def whole(shape):
    return pl.BlockSpec(shape, lambda i, order: (0,) * len(shape))


def run(kernel, order, args, in_specs, out_shape, out_specs, scratch, flops, moved):
    return pl.pallas_call(
        kernel,
        grid_spec=pltpu.PrefetchScalarGridSpec(
            num_scalar_prefetch=1,
            grid=(8,),
            in_specs=in_specs,
            out_specs=out_specs,
            scratch_shapes=scratch,
        ),
        out_shape=out_shape,
        compiler_params=pltpu.CompilerParams(
            dimension_semantics=("arbitrary",), vmem_limit_bytes=24 * 2**20
        ),
        cost_estimate=pl.CostEstimate(flops=flops, bytes_accessed=moved, transcendentals=0),
    )(order, *args)


def on_device(
    stream_first, stream_second, grad_first, grad_second, expert_ids, gate_probs, w_in, w_out
):
    tokens, part = stream_first.shape
    topk = expert_ids.shape[1]
    width = part * 8
    experts = 32
    half = 16
    slots = experts * half
    core = lax.axis_index("core")
    zh = lax.axis_index("zh")

    expert = jnp.arange(experts, dtype=jnp.int32)
    match = expert_ids[:, :, None] == expert[None, None, :]
    named = jnp.any(match, axis=1).astype(BF16)
    earlier = jnp.tri(tokens, k=-1, dtype=BF16)
    before = jnp.dot(earlier, named, preferred_element_type=F32)
    rank = jnp.sum(jnp.where(match, before[:, None, :], 0.0), axis=2).astype(jnp.int32)
    q = jnp.where(rank % 2 == core, expert_ids * half + rank // 2, -1)
    qt = q.T
    gt = gate_probs.T
    lanes = jnp.arange(4, dtype=jnp.int32)
    columns = (jnp.bitwise_xor(zh, lanes)) * 2
    order = jnp.concatenate([columns + core, columns + (1 - core)]).astype(jnp.int32)

    first_parts = gather_features(stream_first)
    second_parts = gather_features(grad_second)

    block = pl.BlockSpec((slots, part), lambda i, order: (0, order[i]))
    token_block = pl.BlockSpec((tokens, part), lambda i, order: (0, order[i]))
    keep_spec = pl.BlockSpec((1, tokens, part), lambda i, order: (jnp.minimum(i, 3), 0, 0))
    give_spec = pl.BlockSpec((1, tokens, part), lambda i, order: (jnp.maximum(i - 4, 0), 0, 0))
    rows_shape = jax.ShapeDtypeStruct((slots, width), BF16)
    full_shape = jax.ShapeDtypeStruct((tokens, width), BF16)
    lane_shape = jax.ShapeDtypeStruct((tokens, 128), F32)
    parts_shape = jax.ShapeDtypeStruct((4, tokens, part), BF16)
    pick_flops = 2 * slots * tokens * width

    rows, first_full, stats = run(
        pack_first_kernel, order, (qt, *first_parts),
        [whole((topk, tokens))] + [whole((tokens, part))] * 8,
        (rows_shape, full_shape, lane_shape),
        (block, token_block, whole((tokens, 128))),
        [pltpu.VMEM((8, tokens, part), BF16), pltpu.VMEM((slots, tokens), BF16)],
        pick_flops, 2 * slots * width,
    )
    send = functools.partial(
        lax.all_to_all, axis_name=CTX, split_axis=0, concat_axis=0, tiled=True
    )
    x = send(rows)
    grad_rows, second_full = run(
        pack_grad_kernel, order, (qt, gt, *second_parts),
        [whole((topk, tokens))] * 2 + [whole((tokens, part))] * 8,
        (rows_shape, full_shape),
        (block, token_block),
        [pltpu.VMEM((slots, tokens), BF16), pltpu.VMEM((slots, 1), F32)],
        pick_flops, 2 * slots * width,
    )
    g = send(grad_rows)

    wi = jnp.concatenate([w_in[0], swap_cores(w_in[0])], axis=1)
    wo = jnp.concatenate([w_out[0], swap_cores(w_out[0])], axis=0)
    own = w_out.shape[1]

    preact = jnp.dot(x, wi, preferred_element_type=F32)
    hidden = gelu_value(preact).astype(BF16)
    result = jnp.dot(hidden, wo, preferred_element_type=F32).astype(BF16)
    back = send(result)
    grad_hidden = lax.dot_general(g, wo, (((1,), (1,)), ((), ())), preferred_element_type=F32)
    grad_pre = (grad_hidden * gelu_slope(preact)).astype(BF16)
    route_dx = lax.dot_general(
        grad_pre, wi, (((1,), (1,)), ((), ())), preferred_element_type=F32
    ).astype(BF16)
    back_dx = send(route_dx)

    rows_rows = (((0,), (0,)), ((), ()))
    out_give = lax.dot_general(hidden[:, own:], g, rows_rows, preferred_element_type=F32).astype(BF16)
    out_got = swap_cores(out_give)
    grad_w_out = lax.dot_general(
        hidden[:, :own], g, rows_rows, preferred_element_type=F32
    ) + out_got.astype(F32)
    in_give = lax.dot_general(x, grad_pre[:, own:], rows_rows, preferred_element_type=F32).astype(BF16)
    in_got = swap_cores(in_give)
    grad_w_in = lax.dot_general(
        x, grad_pre[:, :own], rows_rows, preferred_element_type=F32
    ) + in_got.astype(F32)

    def reduce_parts(keep, give):
        got = swap_cores(give)
        half_sum = [(keep[r].astype(F32) + got[r].astype(F32)) for r in range(4)]
        arrived = [swap_chips(half_sum[r].astype(BF16), r).astype(F32) for r in (1, 2, 3)]
        return half_sum[0] + arrived[0] + arrived[1] + arrived[2]

    keep, give, inner = run(
        combine_out_kernel, order, (q, gate_probs, back, second_full),
        [whole((tokens, topk))] * 2 + [block, token_block],
        (parts_shape, parts_shape, lane_shape),
        (keep_spec, give_spec, whole((tokens, 128))),
        [pltpu.VMEM((tokens, slots), BF16)] * 2 + [pltpu.VMEM((tokens, slots), F32)],
        3 * pick_flops, 2 * slots * width,
    )
    branch = reduce_parts(keep, give)
    stream_input = (stream_second.astype(F32) - branch).astype(BF16)

    keep, give, sums = run(
        combine_dx_kernel, order, (q, inner, stats, back_dx, first_full),
        [whole((tokens, topk))] + [whole((tokens, 128))] * 2 + [block, token_block],
        (parts_shape, parts_shape, lane_shape),
        (keep_spec, give_spec, whole((tokens, 128))),
        [pltpu.VMEM((tokens, slots), BF16), pltpu.VMEM((tokens, 128), F32)],
        pick_flops, 2 * slots * width,
    )
    sums = sums + swap_cores(sums)
    s1, s2, s3 = [swap_chips(sums, r) for r in (1, 2, 3)]
    sums = (sums + s1) + (s2 + s3)
    grad_normed = reduce_parts(keep, give)
    mean, rstd = stats[:, 0:1], stats[:, 1:2]
    normed = (stream_first.astype(F32) - mean) * rstd
    correction = grad_normed - sums[:, 4:5] / width - normed * (sums[:, 5:6] / width)
    grad_stream = (grad_first.astype(F32) + rstd * correction).astype(BF16)
    return stream_input, grad_stream, grad_w_in[None], grad_w_out[None], sums[:, :topk]


def solution(mesh):
    wide = Mesh(
        mesh.devices.reshape(4, 2, 4, 4, 2), ("y", "zl", "x", "zh", "core")
    )
    tp = ("zh", "core")
    in_specs = (
        P(CTX, tp),
        P(CTX, tp),
        P(CTX, tp),
        P(CTX, tp),
        P(CTX, None),
        P(CTX, None),
        P(CTX, None, tp),
        P(CTX, tp, None),
    )
    out_specs = (
        P(CTX, tp),
        P(CTX, tp),
        P(CTX, None, tp),
        P(CTX, tp, None),
        P(CTX, None),
    )
    return jax.shard_map(
        on_device, mesh=wide, in_specs=in_specs, out_specs=out_specs, check_vma=False
    )
```

```python
import functools

import jax
import jax.numpy as jnp
from jax import lax
from jax.experimental import pallas as pl
from jax.experimental.pallas import tpu as pltpu
from jax.sharding import Mesh, PartitionSpec as P

F32 = jnp.float32
BF16 = jnp.bfloat16
CTX = ("y", "zl", "x")
CORES = ((0, 1), (1, 0))


def gelu_value(x):
    return x * 0.5 * (1.0 + lax.erf(x * 0.7071067811865476))


def gelu_slope(x):
    return (
        0.5 * (1.0 + lax.erf(x * 0.7071067811865476))
        + x * jnp.exp(-0.5 * x * x) * 0.3989422804014327
    )


def swap_cores(v):
    return lax.ppermute(v, "core", CORES)


def swap_chips(v, r):
    return lax.ppermute(v, "zh", [(i, i ^ r) for i in range(4)])


def gather_chips(v):
    return [v] + [swap_chips(v, r) for r in (1, 2, 3)]


def gather_features(v):
    mine = gather_chips(v)
    return mine + [swap_cores(m) for m in mine]


def select_rows(qt, slots):
    topk, tokens = qt.shape
    at = lax.broadcasted_iota(jnp.int32, (slots, tokens), 0)
    hit = at == qt[0:1, :]
    for k in range(1, topk):
        hit = jnp.logical_or(hit, at == qt[k : k + 1, :])
    return hit


def columns_of(core, mine, other):
    first = core == 0
    left = jnp.where(first, mine, other)
    right = jnp.where(first, other, mine)
    return jnp.concatenate([left, right], axis=1)


def pack_first_kernel(order, qt_ref, *refs):
    parts, (out_ref, full_ref, stats_ref, low, pick) = refs[:8], refs[8:]
    step = pl.program_id(0)
    core = order[4]

    @pl.when(step == 0)
    def _():
        width = 8 * parts[0].shape[1]
        total = sum(jnp.sum(p[...].astype(F32), axis=1, keepdims=True) for p in parts)
        mean = total / width
        square = sum(
            jnp.sum(jnp.square(p[...].astype(F32) - mean), axis=1, keepdims=True) for p in parts
        )
        rstd = lax.rsqrt(square / width + 1e-05)
        for i in range(4):
            both = columns_of(core, parts[i][...].astype(F32), parts[4 + i][...].astype(F32))
            low[i] = ((both - mean) * rstd).astype(BF16)
        lane = lax.broadcasted_iota(jnp.int32, stats_ref.shape, 1)
        stats_ref[...] = jnp.where(lane == 0, mean, rstd)
        pick[...] = jnp.where(select_rows(qt_ref[...], pick.shape[0]), 1.0, 0.0).astype(BF16)

    for i in range(4):

        @pl.when(step == i)
        def _(i=i):
            full_ref[...] = columns_of(core, parts[i][...].astype(F32), parts[4 + i][...].astype(F32)).astype(BF16)

    out_ref[...] = jnp.dot(pick[...], low[step], preferred_element_type=F32).astype(BF16)


def pack_grad_kernel(order, qt_ref, gt_ref, *refs):
    parts, (out_ref, full_ref, pick, gate) = refs[:8], refs[8:]
    step = pl.program_id(0)
    core = order[4]

    @pl.when(step == 0)
    def _():
        slots = pick.shape[0]
        qt, gt = qt_ref[...], gt_ref[...]
        pick[...] = jnp.where(select_rows(qt, slots), 1.0, 0.0).astype(BF16)
        at = lax.broadcasted_iota(jnp.int32, (slots, qt.shape[1]), 0)
        weight = jnp.zeros((slots, qt.shape[1]), F32)
        for k in range(qt.shape[0]):
            weight = weight + jnp.where(at == qt[k : k + 1, :], gt[k : k + 1, :], 0.0)
        gate[...] = jnp.sum(weight, axis=1, keepdims=True)

    for i in range(4):

        @pl.when(step == i)
        def _(i=i):
            both = columns_of(core, parts[i][...].astype(F32), parts[4 + i][...].astype(F32)).astype(BF16)
            full_ref[...] = both
            rows = jnp.dot(pick[...], both, preferred_element_type=F32)
            out_ref[...] = (gate[...] * rows).astype(BF16)


def combine_out_kernel(order, q_ref, g_ref, rows_ref, full_ref, keep_ref, give_ref, inner_ref, high, rest, inner):
    step = pl.program_id(0)
    part = keep_ref.shape[2]
    first = order[4] == 0

    @pl.when(step == 0)
    def _():
        lane = lax.broadcasted_iota(jnp.int32, inner.shape, 1)
        weight = jnp.zeros(inner.shape, F32)
        for k in range(q_ref.shape[1]):
            weight = weight + jnp.where(lane == q_ref[:, k : k + 1], g_ref[:, k : k + 1], 0.0)
        top = weight.astype(BF16)
        high[...] = top
        rest[...] = (weight - top.astype(F32)).astype(BF16)
        inner[...] = jnp.zeros_like(inner)

    rows = rows_ref[...]
    value = jnp.dot(high[...], rows, preferred_element_type=F32) + jnp.dot(
        rest[...], rows, preferred_element_type=F32
    )
    left, right = value[:, :part], value[:, part:]
    keep_ref[0] = jnp.where(first, left, right).astype(BF16)
    give_ref[0] = jnp.where(first, right, left).astype(BF16)
    inner[...] += lax.dot_general(
        full_ref[...], rows, (((1,), (1,)), ((), ())), preferred_element_type=F32
    )

    @pl.when(step == 3)
    def _():
        lane = lax.broadcasted_iota(jnp.int32, inner.shape, 1)
        place = lax.broadcasted_iota(jnp.int32, inner_ref.shape, 1) % 8
        found = jnp.zeros(inner_ref.shape, F32)
        for k in range(q_ref.shape[1]):
            one = jnp.sum(
                jnp.where(lane == q_ref[:, k : k + 1], inner[...], 0.0), axis=1, keepdims=True
            )
            found = found + jnp.where(place == k, one, 0.0)
        inner_ref[...] = found


def combine_dx_kernel(order, q_ref, inner_ref, stats_ref, rows_ref, full_ref, keep_ref, give_ref, sums_ref, pick, sums):
    step = pl.program_id(0)
    part = keep_ref.shape[2]
    first = order[4] == 0

    @pl.when(step == 0)
    def _():
        lane = lax.broadcasted_iota(jnp.int32, pick.shape, 1)
        hit = lane == q_ref[:, 0:1]
        for k in range(1, q_ref.shape[1]):
            hit = jnp.logical_or(hit, lane == q_ref[:, k : k + 1])
        pick[...] = jnp.where(hit, 1.0, 0.0).astype(BF16)
        sums[...] = inner_ref[...]

    value = jnp.dot(pick[...], rows_ref[...], preferred_element_type=F32)
    left, right = value[:, :part], value[:, part:]
    keep_ref[0] = jnp.where(first, left, right).astype(BF16)
    give_ref[0] = jnp.where(first, right, left).astype(BF16)
    normed = (full_ref[...].astype(F32) - stats_ref[:, 0:1]) * stats_ref[:, 1:2]
    lane = lax.broadcasted_iota(jnp.int32, sums.shape, 1)
    place = lane % 8
    plain = jnp.sum(value, axis=1, keepdims=True)
    mixed = jnp.sum(value * normed, axis=1, keepdims=True)
    sums[...] += jnp.where(place == 4, plain, 0.0) + jnp.where(place == 5, mixed, 0.0)

    @pl.when(step == 3)
    def _():
        all_sums = sums[...]
        high = all_sums.astype(BF16).astype(F32)
        middle = (all_sums - high).astype(BF16).astype(F32)
        lowest = all_sums - high - middle
        sums_ref[...] = jnp.where(lane < 8, high, jnp.where(lane < 16, middle, lowest)).astype(BF16)


def join_thirds(v):
    v = v.astype(F32)
    return (v[:, 0:8] + v[:, 8:16]) + v[:, 16:24]


def split_thirds(v):
    high = lax.reduce_precision(v, 8, 7)
    middle = lax.reduce_precision(v - high, 8, 7)
    lowest = v - high - middle
    return jnp.pad(jnp.concatenate([high, middle, lowest], axis=1).astype(BF16), ((0, 0), (0, 104)))


def whole(shape):
    return pl.BlockSpec(shape, lambda i, order: (0,) * len(shape))


def run(kernel, order, args, in_specs, out_shape, out_specs, scratch, flops, moved, limit=None):
    return pl.pallas_call(
        kernel,
        grid_spec=pltpu.PrefetchScalarGridSpec(
            num_scalar_prefetch=1,
            grid=(4,),
            in_specs=in_specs,
            out_specs=out_specs,
            scratch_shapes=scratch,
        ),
        out_shape=out_shape,
        compiler_params=pltpu.CompilerParams(
            dimension_semantics=("arbitrary",), vmem_limit_bytes=limit
        ),
        cost_estimate=pl.CostEstimate(flops=flops, bytes_accessed=moved, transcendentals=0),
    )(order, *args)


def on_device(
    stream_first, stream_second, grad_first, grad_second, expert_ids, gate_probs, w_in, w_out
):
    tokens, part = stream_first.shape
    topk = expert_ids.shape[1]
    width = part * 8
    experts = 32
    half = 16
    slots = experts * half
    core = lax.axis_index("core")
    zh = lax.axis_index("zh")

    expert = jnp.arange(experts, dtype=jnp.int32)
    match = expert_ids[:, :, None] == expert[None, None, :]
    named = jnp.any(match, axis=1).astype(BF16)
    earlier = jnp.tri(tokens, k=-1, dtype=BF16)
    before = jnp.dot(earlier, named, preferred_element_type=F32)
    rank = jnp.sum(jnp.where(match, before[:, None, :], 0.0), axis=2).astype(jnp.int32)
    q = jnp.where(rank % 2 == core, expert_ids * half + rank // 2, -1)
    qt = q.T
    gt = gate_probs.T
    order = jnp.append(jnp.bitwise_xor(zh, jnp.arange(4, dtype=jnp.int32)), core).astype(jnp.int32)

    first_parts = gather_features(stream_first)
    second_parts = gather_chips(grad_second)

    block = pl.BlockSpec((slots, 2 * part), lambda i, order: (0, order[i]))
    token_block = pl.BlockSpec((tokens, 2 * part), lambda i, order: (0, order[i]))
    step_block = pl.BlockSpec((1, tokens, part), lambda i, order: (i, 0, 0))
    rows_shape = jax.ShapeDtypeStruct((slots, width), BF16)
    full_shape = jax.ShapeDtypeStruct((tokens, width), BF16)
    lane_shape = jax.ShapeDtypeStruct((tokens, 128), F32)
    parts_shape = jax.ShapeDtypeStruct((4, tokens, part), BF16)
    pick_flops = 2 * slots * tokens * width

    rows, first_full, stats = run(
        pack_first_kernel, order, (qt, *first_parts),
        [whole((topk, tokens))] + [whole((tokens, part))] * 8,
        (rows_shape, full_shape, lane_shape),
        (block, token_block, whole((tokens, 128))),
        [pltpu.VMEM((4, tokens, 2 * part), BF16), pltpu.VMEM((slots, tokens), BF16)],
        pick_flops, 2 * slots * width, 24 * 2**20,
    )
    send = functools.partial(
        lax.all_to_all, axis_name=CTX, split_axis=0, concat_axis=0, tiled=True
    )
    rows, *second_parts = lax.optimization_barrier((rows, *second_parts))
    x = send(rows)
    second_parts = second_parts + [swap_cores(p) for p in second_parts]
    grad_rows, second_full = run(
        pack_grad_kernel, order, (qt, gt, *second_parts),
        [whole((topk, tokens))] * 2 + [whole((tokens, part))] * 8,
        (rows_shape, full_shape),
        (block, token_block),
        [pltpu.VMEM((slots, tokens), BF16), pltpu.VMEM((slots, 1), F32)],
        pick_flops, 2 * slots * width, 24 * 2**20,
    )
    g = send(grad_rows)

    wi = jnp.concatenate([w_in[0], swap_cores(w_in[0])], axis=1)
    wo = jnp.concatenate([w_out[0], swap_cores(w_out[0])], axis=0)
    own = w_out.shape[1]

    preact = jnp.dot(x, wi, preferred_element_type=F32)
    hidden = gelu_value(preact).astype(BF16)
    result = jnp.dot(hidden, wo, preferred_element_type=F32).astype(BF16)
    back = send(result)
    grad_hidden = lax.dot_general(g, wo, (((1,), (1,)), ((), ())), preferred_element_type=F32)
    grad_pre = (grad_hidden * gelu_slope(preact)).astype(BF16)
    route_dx = lax.dot_general(
        grad_pre, wi, (((1,), (1,)), ((), ())), preferred_element_type=F32
    ).astype(BF16)
    back_dx = send(route_dx)

    keep_out, give_out, inner = run(
        combine_out_kernel, order, (q, gate_probs, back, second_full),
        [whole((tokens, topk))] * 2 + [block, token_block],
        (parts_shape, parts_shape, lane_shape),
        (step_block, step_block, whole((tokens, 128))),
        [pltpu.VMEM((tokens, slots), BF16)] * 2 + [pltpu.VMEM((tokens, slots), F32)],
        3 * pick_flops, 2 * slots * width,
    )
    got_out = swap_cores(give_out)
    half_out = [keep_out[r].astype(F32) + got_out[r].astype(F32) for r in range(4)]

    rows_rows = (((0,), (0,)), ((), ()))
    out_give = lax.dot_general(hidden[:, own:], g, rows_rows, preferred_element_type=F32).astype(BF16)
    out_got = swap_cores(out_give)
    grad_w_out = lax.dot_general(
        hidden[:, :own], g, rows_rows, preferred_element_type=F32
    ) + out_got.astype(F32)
    in_give = lax.dot_general(x, grad_pre[:, own:], rows_rows, preferred_element_type=F32).astype(BF16)
    in_got = swap_cores(in_give)
    grad_w_in = lax.dot_general(
        x, grad_pre[:, :own], rows_rows, preferred_element_type=F32
    ) + in_got.astype(F32)

    back_dx, half_out, grad_w_in, grad_w_out = lax.optimization_barrier(
        (back_dx, half_out, grad_w_in, grad_w_out)
    )
    keep, give, sums = run(
        combine_dx_kernel, order, (q, inner, stats, back_dx, first_full),
        [whole((tokens, topk))] + [whole((tokens, 128))] * 2 + [block, token_block],
        (parts_shape, parts_shape, jax.ShapeDtypeStruct((tokens, 128), BF16)),
        (step_block, step_block, whole((tokens, 128))),
        [pltpu.VMEM((tokens, slots), BF16), pltpu.VMEM((tokens, 128), F32)],
        pick_flops, 2 * slots * width, 24 * 2**20,
    )
    got, got_sums = swap_cores(give), swap_cores(sums)
    half_sum = [keep[r].astype(F32) + got[r].astype(F32) for r in range(4)]
    sums = join_thirds(sums) + join_thirds(got_sums)
    thirds = split_thirds(sums)
    others = [
        swap_chips(
            jnp.concatenate([half_sum[r].astype(BF16), half_out[r].astype(BF16), thirds], axis=1), r
        )
        for r in (1, 2, 3)
    ]
    s1, s2, s3 = [join_thirds(o[:, 2 * part :]) for o in others]
    sums = (sums + s1) + (s2 + s3)
    grad_normed, branch = half_sum[0], half_out[0]
    for o in others:
        grad_normed = grad_normed + o[:, :part].astype(F32)
        branch = branch + o[:, part : 2 * part].astype(F32)
    stream_input = (stream_second.astype(F32) - branch).astype(BF16)
    mean, rstd = stats[:, 0:1], stats[:, 1:2]
    normed = (stream_first.astype(F32) - mean) * rstd
    correction = grad_normed - sums[:, 4:5] / width - normed * (sums[:, 5:6] / width)
    grad_stream = (grad_first.astype(F32) + rstd * correction).astype(BF16)
    return stream_input, grad_stream, grad_w_in[None], grad_w_out[None], sums[:, :topk]


def solution(mesh):
    wide = Mesh(
        mesh.devices.reshape(4, 2, 4, 4, 2), ("y", "zl", "x", "zh", "core")
    )
    tp = ("zh", "core")
    in_specs = (
        P(CTX, tp),
        P(CTX, tp),
        P(CTX, tp),
        P(CTX, tp),
        P(CTX, None),
        P(CTX, None),
        P(CTX, None, tp),
        P(CTX, tp, None),
    )
    out_specs = (
        P(CTX, tp),
        P(CTX, tp),
        P(CTX, None, tp),
        P(CTX, tp, None),
        P(CTX, None),
    )
    return jax.shard_map(
        on_device, mesh=wide, in_specs=in_specs, out_specs=out_specs, check_vma=False
    )
```

```python
import functools

import jax
import jax.numpy as jnp
from jax import lax
from jax.experimental import pallas as pl
from jax.experimental.pallas import tpu as pltpu
from jax.sharding import Mesh, PartitionSpec as P

F32 = jnp.float32
BF16 = jnp.bfloat16
CTX = ("y", "zl", "x")
CORES = ((0, 1), (1, 0))


def gelu_value(x):
    return x * 0.5 * (1.0 + lax.erf(x * 0.7071067811865476))


def gelu_slope(x):
    return (
        0.5 * (1.0 + lax.erf(x * 0.7071067811865476))
        + x * jnp.exp(-0.5 * x * x) * 0.3989422804014327
    )


def swap_cores(v):
    return lax.ppermute(v, "core", CORES)


def swap_chips(v, r):
    return lax.ppermute(v, "zh", [(i, i ^ r) for i in range(4)])


def gather_chips(v):
    return [v] + [swap_chips(v, r) for r in (1, 2, 3)]


def gather_features(v):
    mine = gather_chips(v)
    return mine + [swap_cores(m) for m in mine]


def select_rows(qt, slots):
    topk, tokens = qt.shape
    at = lax.broadcasted_iota(jnp.int32, (slots, tokens), 0)
    hit = at == qt[0:1, :]
    for k in range(1, topk):
        hit = jnp.logical_or(hit, at == qt[k : k + 1, :])
    return hit


def columns_of(core, mine, other):
    first = core == 0
    left = jnp.where(first, mine, other)
    right = jnp.where(first, other, mine)
    return jnp.concatenate([left, right], axis=1)


def pack_kernel(order, qt_ref, gt_ref, *refs):
    parts, (out_ref, first_ref, second_ref, stats_ref, low, pick, gate) = refs[:8], refs[8:]
    step = pl.program_id(0)
    core = order[4]
    slots = pick.shape[0]
    half = out_ref.shape[1] // 2

    @pl.when(step == 0)
    def _():
        width = 8 * parts[0].shape[2]
        total = sum(jnp.sum(p[0].astype(F32), axis=1, keepdims=True) for p in parts)
        mean = total / width
        square = sum(
            jnp.sum(jnp.square(p[0].astype(F32) - mean), axis=1, keepdims=True) for p in parts
        )
        rstd = lax.rsqrt(square / width + 1e-05)
        for i in range(4):
            both = columns_of(core, parts[i][0].astype(F32), parts[4 + i][0].astype(F32))
            low[i] = ((both - mean) * rstd).astype(BF16)
        lane = lax.broadcasted_iota(jnp.int32, stats_ref.shape, 1)
        stats_ref[...] = jnp.where(lane == 0, mean, rstd)
        qt, gt = qt_ref[...], gt_ref[...]
        pick[...] = jnp.where(select_rows(qt, slots), 1.0, 0.0).astype(BF16)
        at = lax.broadcasted_iota(jnp.int32, (slots, qt.shape[1]), 0)
        weight = jnp.zeros((slots, qt.shape[1]), F32)
        for k in range(qt.shape[0]):
            weight = weight + jnp.where(at == qt[k : k + 1, :], gt[k : k + 1, :], 0.0)
        gate[...] = jnp.sum(weight, axis=1, keepdims=True)

    rows = jnp.dot(pick[...], low[step], preferred_element_type=F32).astype(BF16)
    out_ref[:, :half, :] = rows.reshape(-1, half, rows.shape[1])

    for i in range(4):

        @pl.when(step == i)
        def _(i=i):
            mine, other = parts[i], parts[4 + i]
            first_ref[...] = columns_of(core, mine[0].astype(F32), other[0].astype(F32)).astype(BF16)
            both = columns_of(core, mine[1].astype(F32), other[1].astype(F32)).astype(BF16)
            second_ref[...] = both
            raw = jnp.dot(pick[...], both, preferred_element_type=F32)
            scaled = (gate[...] * raw).astype(BF16)
            out_ref[:, half:, :] = scaled.reshape(-1, half, scaled.shape[1])


def expert_kernel(x_ref, g_ref, wi_a, wi_b, wo_a, wo_b, out_ref, hidden_ref, pre_ref):
    blocks, half, width = x_ref.shape
    own = wi_a.shape[1]
    wide = width // 4
    x = x_ref[...].reshape(blocks * half, width)
    g = g_ref[...].reshape(blocks * half, width)
    last = (((1,), (1,)), ((), ()))
    hidden, grad_pre = [], []
    for wi, wo in ((wi_a, wo_a), (wi_b, wo_b)):
        preact = jnp.dot(x, wi[...], preferred_element_type=F32)
        hidden.append(gelu_value(preact).astype(BF16))
        grad_hidden = lax.dot_general(g, wo[...], last, preferred_element_type=F32)
        grad_pre.append((grad_hidden * gelu_slope(preact)).astype(BF16))
    hidden_ref[:, :own], hidden_ref[:, own:] = hidden
    pre_ref[:, :own], pre_ref[:, own:] = grad_pre
    for n in range(4):
        at = slice(n * wide, (n + 1) * wide)
        value = jnp.dot(hidden[0], wo_a[:, at], preferred_element_type=F32) + jnp.dot(
            hidden[1], wo_b[:, at], preferred_element_type=F32
        )
        out_ref[:, :half, at] = value.astype(BF16).reshape(blocks, half, wide)
        value = lax.dot_general(
            grad_pre[0], wi_a[at, :], last, preferred_element_type=F32
        ) + lax.dot_general(grad_pre[1], wi_b[at, :], last, preferred_element_type=F32)
        out_ref[:, half:, at] = value.astype(BF16).reshape(blocks, half, wide)


def combine_kernel(order, q_ref, g_ref, stats_ref, out_rows, dx_rows, first_ref, second_ref, keep_ref, give_ref, sums_ref, high, rest, pick, inner, sums):
    step = pl.program_id(0)
    part = keep_ref.shape[2] // 2
    slots = pick.shape[1]
    topk = q_ref.shape[1]
    first = order[4] == 0

    @pl.when(step == 0)
    def _():
        lane = lax.broadcasted_iota(jnp.int32, inner.shape, 1)
        weight = jnp.zeros(inner.shape, F32)
        for k in range(topk):
            weight = weight + jnp.where(lane == q_ref[:, k : k + 1], g_ref[:, k : k + 1], 0.0)
        top = weight.astype(BF16)
        high[...] = top
        rest[...] = (weight - top.astype(F32)).astype(BF16)
        hit = lane == q_ref[:, 0:1]
        for k in range(1, topk):
            hit = jnp.logical_or(hit, lane == q_ref[:, k : k + 1])
        pick[...] = jnp.where(hit, 1.0, 0.0).astype(BF16)
        inner[...] = jnp.zeros_like(inner)
        sums[...] = jnp.zeros_like(sums)

    def store(value, at):
        left, right = value[:, :part], value[:, part:]
        keep_ref[0, :, at : at + part] = jnp.where(first, left, right).astype(BF16)
        give_ref[0, :, at : at + part] = jnp.where(first, right, left).astype(BF16)

    rows = out_rows[...].reshape(slots, 2 * part)
    value = jnp.dot(high[...], rows, preferred_element_type=F32) + jnp.dot(
        rest[...], rows, preferred_element_type=F32
    )
    store(value, 0)
    inner[...] += lax.dot_general(
        second_ref[...], rows, (((1,), (1,)), ((), ())), preferred_element_type=F32
    )
    value = jnp.dot(pick[...], dx_rows[...].reshape(slots, 2 * part), preferred_element_type=F32)
    store(value, part)
    normed = (first_ref[...].astype(F32) - stats_ref[:, 0:1]) * stats_ref[:, 1:2]
    lane = lax.broadcasted_iota(jnp.int32, sums.shape, 1)
    place = lane % 8
    plain = jnp.sum(value, axis=1, keepdims=True)
    mixed = jnp.sum(value * normed, axis=1, keepdims=True)
    sums[...] += jnp.where(place == 4, plain, 0.0) + jnp.where(place == 5, mixed, 0.0)

    @pl.when(step == 3)
    def _():
        slot = lax.broadcasted_iota(jnp.int32, inner.shape, 1)
        all_sums = sums[...]
        for k in range(topk):
            one = jnp.sum(
                jnp.where(slot == q_ref[:, k : k + 1], inner[...], 0.0), axis=1, keepdims=True
            )
            all_sums = all_sums + jnp.where(place == k, one, 0.0)
        top = all_sums.astype(BF16).astype(F32)
        middle = (all_sums - top).astype(BF16).astype(F32)
        lowest = all_sums - top - middle
        sums_ref[...] = jnp.where(lane < 8, top, jnp.where(lane < 16, middle, lowest)).astype(BF16)


def join_thirds(v):
    v = v.astype(F32)
    return (v[:, 0:8] + v[:, 8:16]) + v[:, 16:24]


def split_thirds(v):
    high = lax.reduce_precision(v, 8, 7)
    middle = lax.reduce_precision(v - high, 8, 7)
    lowest = v - high - middle
    return jnp.pad(jnp.concatenate([high, middle, lowest], axis=1).astype(BF16), ((0, 0), (0, 104)))


def whole(shape):
    return pl.BlockSpec(shape, lambda i, order: (0,) * len(shape))


def run(kernel, order, args, in_specs, out_shape, out_specs, scratch, flops, moved, limit=None):
    return pl.pallas_call(
        kernel,
        grid_spec=pltpu.PrefetchScalarGridSpec(
            num_scalar_prefetch=1,
            grid=(4,),
            in_specs=in_specs,
            out_specs=out_specs,
            scratch_shapes=scratch,
        ),
        out_shape=out_shape,
        compiler_params=pltpu.CompilerParams(
            dimension_semantics=("arbitrary",), vmem_limit_bytes=limit
        ),
        cost_estimate=pl.CostEstimate(flops=flops, bytes_accessed=moved, transcendentals=0),
    )(order, *args)


def on_device(
    stream_first, stream_second, grad_first, grad_second, expert_ids, gate_probs, w_in, w_out
):
    tokens, part = stream_first.shape
    topk = expert_ids.shape[1]
    width = part * 8
    experts = 32
    half = 16
    slots = experts * half
    core = lax.axis_index("core")
    zh = lax.axis_index("zh")

    expert = jnp.arange(experts, dtype=jnp.int32)
    match = expert_ids[:, :, None] == expert[None, None, :]
    named = jnp.any(match, axis=1).astype(BF16)
    earlier = jnp.tri(tokens, k=-1, dtype=BF16)
    before = jnp.dot(earlier, named, preferred_element_type=F32)
    rank = jnp.sum(jnp.where(match, before[:, None, :], 0.0), axis=2).astype(jnp.int32)
    q = jnp.where(rank % 2 == core, expert_ids * half + rank // 2, -1)
    qt = q.T
    gt = gate_probs.T
    order = jnp.append(jnp.bitwise_xor(zh, jnp.arange(4, dtype=jnp.int32)), core).astype(jnp.int32)

    streams = gather_features(jnp.stack([stream_first, grad_second]))

    token_block = pl.BlockSpec((tokens, 2 * part), lambda i, order: (0, order[i]))
    step_block = pl.BlockSpec((1, tokens, 2 * part), lambda i, order: (i, 0, 0))
    rows_shape = jax.ShapeDtypeStruct((experts, 2 * half, width), BF16)
    full_shape = jax.ShapeDtypeStruct((tokens, width), BF16)
    lane_shape = jax.ShapeDtypeStruct((tokens, 128), F32)
    parts_shape = jax.ShapeDtypeStruct((4, tokens, 2 * part), BF16)
    pick_flops = 2 * slots * tokens * width

    def rows_block(n):
        return pl.BlockSpec((experts, half, 2 * part), lambda i, order: (0, n, order[i]))

    rows, first_full, second_full, stats = run(
        pack_kernel, order, (qt, gt, *streams),
        [whole((topk, tokens))] * 2 + [whole((2, tokens, part))] * 8,
        (rows_shape, full_shape, full_shape, lane_shape),
        (
            pl.BlockSpec((experts, 2 * half, 2 * part), lambda i, order: (0, 0, order[i])),
            token_block, token_block, whole((tokens, 128)),
        ),
        [
            pltpu.VMEM((4, tokens, 2 * part), BF16),
            pltpu.VMEM((slots, tokens), BF16),
            pltpu.VMEM((slots, 1), F32),
        ],
        2 * pick_flops, 4 * slots * width, 24 * 2**20,
    )
    send = functools.partial(
        lax.all_to_all, axis_name=CTX, split_axis=0, concat_axis=0, tiled=True
    )
    wi, wo = w_in[0], w_out[0]
    gates = jnp.pad(gate_probs, ((0, 0), (0, 128 - topk)))
    rows, gates, wi_b, wo_b = lax.optimization_barrier(
        (rows, gates, swap_cores(wi), swap_cores(wo))
    )
    arrived = send(rows)

    own = wo.shape[0]
    step_rows = experts // 2

    def source_block(n):
        return pl.BlockSpec((step_rows, half, width), lambda i: (i, n, 0))

    def fixed(shape):
        return pl.BlockSpec(shape, lambda i: (0, 0))

    unit_block = pl.BlockSpec((step_rows * half, 2 * own), lambda i: (i, 0))
    unit_shape = jax.ShapeDtypeStruct((slots, 2 * own), BF16)
    results, hidden, grad_pre = pl.pallas_call(
        expert_kernel,
        grid=(2,),
        in_specs=[
            source_block(0), source_block(1),
            fixed((width, own)), fixed((width, own)), fixed((own, width)), fixed((own, width)),
        ],
        out_specs=(
            pl.BlockSpec((step_rows, 2 * half, width), lambda i: (i, 0, 0)), unit_block, unit_block
        ),
        out_shape=(rows_shape, unit_shape, unit_shape),
        compiler_params=pltpu.CompilerParams(
            dimension_semantics=("arbitrary",), vmem_limit_bytes=60 * 2**20
        ),
        cost_estimate=pl.CostEstimate(
            flops=16 * slots * own * width, bytes_accessed=12 * slots * width, transcendentals=0
        ),
    )(arrived, arrived, wi, wi_b, wo, wo_b)
    back = send(results)

    keep, give, sums = run(
        combine_kernel, order, (q, gates, stats, back, back, first_full, second_full),
        [whole((tokens, topk))]
        + [whole((tokens, 128))] * 2
        + [rows_block(0), rows_block(1), token_block, token_block],
        (parts_shape, parts_shape, jax.ShapeDtypeStruct((tokens, 128), BF16)),
        (step_block, step_block, whole((tokens, 128))),
        [pltpu.VMEM((tokens, slots), BF16)] * 3
        + [pltpu.VMEM((tokens, slots), F32), pltpu.VMEM((tokens, 128), F32)],
        4 * pick_flops, 4 * slots * width, 24 * 2**20,
    )
    got, got_sums = swap_cores(give), swap_cores(sums)
    halves = [keep[r].astype(F32) + got[r].astype(F32) for r in range(4)]
    sums = join_thirds(sums) + join_thirds(got_sums)
    thirds = split_thirds(sums)
    sent = [jnp.concatenate([halves[r].astype(BF16), thirds], axis=1) for r in (1, 2, 3)]
    arrived, hidden, grad_pre, *sent = lax.optimization_barrier((arrived, hidden, grad_pre, *sent))
    others = [swap_chips(v, r) for r, v in zip((1, 2, 3), sent)]

    x = arrived[:, :half].reshape(slots, width)
    g = arrived[:, half:].reshape(slots, width)
    rows_rows = (((0,), (0,)), ((), ()))
    out_give = lax.dot_general(hidden[:, own:], g, rows_rows, preferred_element_type=F32).astype(BF16)
    out_got = swap_cores(out_give)
    grad_w_out = lax.dot_general(
        hidden[:, :own], g, rows_rows, preferred_element_type=F32
    ) + out_got.astype(F32)
    in_give = lax.dot_general(x, grad_pre[:, own:], rows_rows, preferred_element_type=F32).astype(BF16)
    in_got = swap_cores(in_give)
    grad_w_in = lax.dot_general(
        x, grad_pre[:, :own], rows_rows, preferred_element_type=F32
    ) + in_got.astype(F32)

    *others, grad_w_in, grad_w_out = lax.optimization_barrier((*others, grad_w_in, grad_w_out))
    s1, s2, s3 = [join_thirds(o[:, 2 * part :]) for o in others]
    sums = (sums + s1) + (s2 + s3)
    total = halves[0]
    for o in others:
        total = total + o[:, : 2 * part].astype(F32)
    branch, grad_normed = total[:, :part], total[:, part:]
    stream_input = (stream_second.astype(F32) - branch).astype(BF16)
    mean, rstd = stats[:, 0:1], stats[:, 1:2]
    normed = (stream_first.astype(F32) - mean) * rstd
    correction = grad_normed - sums[:, 4:5] / width - normed * (sums[:, 5:6] / width)
    grad_stream = (grad_first.astype(F32) + rstd * correction).astype(BF16)
    return stream_input, grad_stream, grad_w_in[None], grad_w_out[None], sums[:, :topk]


def solution(mesh):
    wide = Mesh(
        mesh.devices.reshape(4, 2, 4, 4, 2), ("y", "zl", "x", "zh", "core")
    )
    tp = ("zh", "core")
    in_specs = (
        P(CTX, tp),
        P(CTX, tp),
        P(CTX, tp),
        P(CTX, tp),
        P(CTX, None),
        P(CTX, None),
        P(CTX, None, tp),
        P(CTX, tp, None),
    )
    out_specs = (
        P(CTX, tp),
        P(CTX, tp),
        P(CTX, None, tp),
        P(CTX, tp, None),
        P(CTX, None),
    )
    return jax.shard_map(
        on_device, mesh=wide, in_specs=in_specs, out_specs=out_specs, check_vma=False
    )
```

```python
import functools

import jax
import jax.numpy as jnp
from jax import lax
from jax.experimental import pallas as pl
from jax.experimental.pallas import tpu as pltpu
from jax.sharding import Mesh, PartitionSpec as P

F32 = jnp.float32
BF16 = jnp.bfloat16
CTX = ("y", "zl", "x")
CORES = ((0, 1), (1, 0))


def gelu_value(x):
    return x * 0.5 * (1.0 + lax.erf(x * 0.7071067811865476))


def gelu_slope(x):
    return (
        0.5 * (1.0 + lax.erf(x * 0.7071067811865476))
        + x * jnp.exp(-0.5 * x * x) * 0.3989422804014327
    )


def swap_cores(v):
    return lax.ppermute(v, "core", CORES)


def swap_chips(v, r):
    return lax.ppermute(v, "zh", [(i, i ^ r) for i in range(4)])


def gather_chips(v):
    return [v] + [swap_chips(v, r) for r in (1, 2, 3)]


def gather_features(v):
    mine = gather_chips(v)
    return mine + [swap_cores(m) for m in mine]


def select_rows(qt, slots):
    topk, tokens = qt.shape
    at = lax.broadcasted_iota(jnp.int32, (slots, tokens), 0)
    hit = at == qt[0:1, :]
    for k in range(1, topk):
        hit = jnp.logical_or(hit, at == qt[k : k + 1, :])
    return hit


def columns_of(core, mine, other):
    first = core == 0
    left = jnp.where(first, mine, other)
    right = jnp.where(first, other, mine)
    return jnp.concatenate([left, right], axis=1)


def pack_kernel(order, qt_ref, gt_ref, *refs):
    parts, (out_ref, first_ref, second_ref, stats_ref, low, pick, gate) = refs[:8], refs[8:]
    step = pl.program_id(0)
    core = order[4]
    slots = pick.shape[0]
    half = out_ref.shape[1] // 2

    @pl.when(step == 0)
    def _():
        width = 8 * parts[0].shape[2]
        total = sum(jnp.sum(p[0].astype(F32), axis=1, keepdims=True) for p in parts)
        mean = total / width
        square = sum(
            jnp.sum(jnp.square(p[0].astype(F32) - mean), axis=1, keepdims=True) for p in parts
        )
        rstd = lax.rsqrt(square / width + 1e-05)
        for i in range(4):
            both = columns_of(core, parts[i][0].astype(F32), parts[4 + i][0].astype(F32))
            low[i] = ((both - mean) * rstd).astype(BF16)
        lane = lax.broadcasted_iota(jnp.int32, stats_ref.shape, 1)
        stats_ref[...] = jnp.where(lane == 0, mean, rstd)
        qt, gt = qt_ref[...], gt_ref[...]
        pick[...] = jnp.where(select_rows(qt, slots), 1.0, 0.0).astype(BF16)
        at = lax.broadcasted_iota(jnp.int32, (slots, qt.shape[1]), 0)
        weight = jnp.zeros((slots, qt.shape[1]), F32)
        for k in range(qt.shape[0]):
            weight = weight + jnp.where(at == qt[k : k + 1, :], gt[k : k + 1, :], 0.0)
        gate[...] = jnp.sum(weight, axis=1, keepdims=True)

    rows = jnp.dot(pick[...], low[step], preferred_element_type=F32).astype(BF16)
    out_ref[:, :half, :] = rows.reshape(-1, half, rows.shape[1])

    for i in range(4):

        @pl.when(step == i)
        def _(i=i):
            mine, other = parts[i], parts[4 + i]
            first_ref[...] = columns_of(core, mine[0].astype(F32), other[0].astype(F32)).astype(BF16)
            both = columns_of(core, mine[1].astype(F32), other[1].astype(F32)).astype(BF16)
            second_ref[...] = both
            raw = jnp.dot(pick[...], both, preferred_element_type=F32)
            scaled = (gate[...] * raw).astype(BF16)
            out_ref[:, half:, :] = scaled.reshape(-1, half, scaled.shape[1])


def expert_kernel(x_ref, g_ref, wi_a, wi_b, wo_a, wo_b, out_ref, hidden_ref, pre_ref):
    blocks, half, width = x_ref.shape
    own = wi_a.shape[1]
    wide = width // 4
    x = x_ref[...].reshape(blocks * half, width)
    g = g_ref[...].reshape(blocks * half, width)
    last = (((1,), (1,)), ((), ()))
    hidden, grad_pre = [], []
    for wi, wo in ((wi_a, wo_a), (wi_b, wo_b)):
        preact = jnp.dot(x, wi[...], preferred_element_type=F32)
        hidden.append(gelu_value(preact).astype(BF16))
        grad_hidden = lax.dot_general(g, wo[...], last, preferred_element_type=F32)
        grad_pre.append((grad_hidden * gelu_slope(preact)).astype(BF16))
    hidden_ref[:, :own], hidden_ref[:, own:] = hidden
    pre_ref[:, :own], pre_ref[:, own:] = grad_pre
    for n in range(4):
        at = slice(n * wide, (n + 1) * wide)
        value = jnp.dot(hidden[0], wo_a[:, at], preferred_element_type=F32) + jnp.dot(
            hidden[1], wo_b[:, at], preferred_element_type=F32
        )
        out_ref[:, :half, at] = value.astype(BF16).reshape(blocks, half, wide)
        value = lax.dot_general(
            grad_pre[0], wi_a[at, :], last, preferred_element_type=F32
        ) + lax.dot_general(grad_pre[1], wi_b[at, :], last, preferred_element_type=F32)
        out_ref[:, half:, at] = value.astype(BF16).reshape(blocks, half, wide)


def combine_kernel(order, q_ref, g_ref, stats_ref, out_rows, dx_rows, first_ref, second_ref, keep_ref, give_ref, sums_ref, high, rest, pick, inner, sums):
    step = pl.program_id(0)
    part = keep_ref.shape[2] // 2
    slots = pick.shape[1]
    topk = q_ref.shape[1]
    first = order[4] == 0

    @pl.when(step == 0)
    def _():
        lane = lax.broadcasted_iota(jnp.int32, inner.shape, 1)
        weight = jnp.zeros(inner.shape, F32)
        for k in range(topk):
            weight = weight + jnp.where(lane == q_ref[:, k : k + 1], g_ref[:, k : k + 1], 0.0)
        top = weight.astype(BF16)
        high[...] = top
        rest[...] = (weight - top.astype(F32)).astype(BF16)
        hit = lane == q_ref[:, 0:1]
        for k in range(1, topk):
            hit = jnp.logical_or(hit, lane == q_ref[:, k : k + 1])
        pick[...] = jnp.where(hit, 1.0, 0.0).astype(BF16)
        inner[...] = jnp.zeros_like(inner)
        sums[...] = jnp.zeros_like(sums)

    def store(value, at):
        left, right = value[:, :part], value[:, part:]
        keep_ref[0, :, at : at + part] = jnp.where(first, left, right).astype(BF16)
        give_ref[0, :, at : at + part] = jnp.where(first, right, left).astype(BF16)

    rows = out_rows[...].reshape(slots, 2 * part)
    value = jnp.dot(high[...], rows, preferred_element_type=F32) + jnp.dot(
        rest[...], rows, preferred_element_type=F32
    )
    store(value, 0)
    inner[...] += lax.dot_general(
        second_ref[...], rows, (((1,), (1,)), ((), ())), preferred_element_type=F32
    )
    value = jnp.dot(pick[...], dx_rows[...].reshape(slots, 2 * part), preferred_element_type=F32)
    store(value, part)
    normed = (first_ref[...].astype(F32) - stats_ref[:, 0:1]) * stats_ref[:, 1:2]
    lane = lax.broadcasted_iota(jnp.int32, sums.shape, 1)
    place = lane % 8
    plain = jnp.sum(value, axis=1, keepdims=True)
    mixed = jnp.sum(value * normed, axis=1, keepdims=True)
    sums[...] += jnp.where(place == 4, plain, 0.0) + jnp.where(place == 5, mixed, 0.0)

    @pl.when(step == 3)
    def _():
        slot = lax.broadcasted_iota(jnp.int32, inner.shape, 1)
        all_sums = sums[...]
        for k in range(topk):
            one = jnp.sum(
                jnp.where(slot == q_ref[:, k : k + 1], inner[...], 0.0), axis=1, keepdims=True
            )
            all_sums = all_sums + jnp.where(place == k, one, 0.0)
        top = all_sums.astype(BF16).astype(F32)
        middle = (all_sums - top).astype(BF16).astype(F32)
        lowest = all_sums - top - middle
        sums_ref[...] = jnp.where(lane < 8, top, jnp.where(lane < 16, middle, lowest)).astype(BF16)


def join_thirds(v):
    v = v.astype(F32)
    return (v[:, 0:8] + v[:, 8:16]) + v[:, 16:24]


def split_thirds(v):
    high = lax.reduce_precision(v, 8, 7)
    middle = lax.reduce_precision(v - high, 8, 7)
    lowest = v - high - middle
    return jnp.pad(jnp.concatenate([high, middle, lowest], axis=1).astype(BF16), ((0, 0), (0, 104)))


def whole(shape):
    return pl.BlockSpec(shape, lambda i, order: (0,) * len(shape))


def run(kernel, order, args, in_specs, out_shape, out_specs, scratch, flops, moved, limit=None):
    return pl.pallas_call(
        kernel,
        grid_spec=pltpu.PrefetchScalarGridSpec(
            num_scalar_prefetch=1,
            grid=(4,),
            in_specs=in_specs,
            out_specs=out_specs,
            scratch_shapes=scratch,
        ),
        out_shape=out_shape,
        compiler_params=pltpu.CompilerParams(
            dimension_semantics=("arbitrary",), vmem_limit_bytes=limit
        ),
        cost_estimate=pl.CostEstimate(flops=flops, bytes_accessed=moved, transcendentals=0),
    )(order, *args)


def on_device(
    stream_first, stream_second, grad_first, grad_second, expert_ids, gate_probs, w_in, w_out
):
    tokens, part = stream_first.shape
    topk = expert_ids.shape[1]
    width = part * 8
    experts = 32
    half = 16
    slots = experts * half
    core = lax.axis_index("core")
    zh = lax.axis_index("zh")

    expert = jnp.arange(experts, dtype=jnp.int32)
    match = expert_ids[:, :, None] == expert[None, None, :]
    named = jnp.any(match, axis=1).astype(BF16)
    earlier = jnp.tri(tokens, k=-1, dtype=BF16)
    before = jnp.dot(earlier, named, preferred_element_type=F32)
    rank = jnp.sum(jnp.where(match, before[:, None, :], 0.0), axis=2).astype(jnp.int32)
    q = jnp.where(rank % 2 == core, expert_ids * half + rank // 2, -1)
    qt = q.T
    gt = gate_probs.T
    order = jnp.append(jnp.bitwise_xor(zh, jnp.arange(4, dtype=jnp.int32)), core).astype(jnp.int32)

    streams = gather_features(jnp.stack([stream_first, grad_second]))

    token_block = pl.BlockSpec((tokens, 2 * part), lambda i, order: (0, order[i]))
    step_block = pl.BlockSpec((1, tokens, 2 * part), lambda i, order: (i, 0, 0))
    rows_shape = jax.ShapeDtypeStruct((experts, 2 * half, width), BF16)
    full_shape = jax.ShapeDtypeStruct((tokens, width), BF16)
    lane_shape = jax.ShapeDtypeStruct((tokens, 128), F32)
    parts_shape = jax.ShapeDtypeStruct((4, tokens, 2 * part), BF16)
    pick_flops = 2 * slots * tokens * width

    def rows_block(n):
        return pl.BlockSpec((experts, half, 2 * part), lambda i, order: (0, n, order[i]))

    rows, first_full, second_full, stats = run(
        pack_kernel, order, (qt, gt, *streams),
        [whole((topk, tokens))] * 2 + [whole((2, tokens, part))] * 8,
        (rows_shape, full_shape, full_shape, lane_shape),
        (
            pl.BlockSpec((experts, 2 * half, 2 * part), lambda i, order: (0, 0, order[i])),
            token_block, token_block, whole((tokens, 128)),
        ),
        [
            pltpu.VMEM((4, tokens, 2 * part), BF16),
            pltpu.VMEM((slots, tokens), BF16),
            pltpu.VMEM((slots, 1), F32),
        ],
        2 * pick_flops, 4 * slots * width, 24 * 2**20,
    )
    send = functools.partial(
        lax.all_to_all, axis_name=CTX, split_axis=0, concat_axis=0, tiled=True
    )
    wi, wo = w_in[0], w_out[0]
    gates = jnp.pad(gate_probs, ((0, 0), (0, 128 - topk)))
    rows, gates, wi_b, wo_b = lax.optimization_barrier(
        (rows, gates, swap_cores(wi), swap_cores(wo))
    )
    arrived = send(rows)

    own = wo.shape[0]
    step_rows = experts // 2

    def source_block(n):
        return pl.BlockSpec((step_rows, half, width), lambda i: (i, n, 0))

    def fixed(shape):
        return pl.BlockSpec(shape, lambda i: (0, 0))

    unit_block = pl.BlockSpec((step_rows * half, 2 * own), lambda i: (i, 0))
    unit_shape = jax.ShapeDtypeStruct((slots, 2 * own), BF16)
    results, hidden, grad_pre = pl.pallas_call(
        expert_kernel,
        grid=(2,),
        in_specs=[
            source_block(0), source_block(1),
            fixed((width, own)), fixed((width, own)), fixed((own, width)), fixed((own, width)),
        ],
        out_specs=(
            pl.BlockSpec((step_rows, 2 * half, width), lambda i: (i, 0, 0)), unit_block, unit_block
        ),
        out_shape=(rows_shape, unit_shape, unit_shape),
        compiler_params=pltpu.CompilerParams(
            dimension_semantics=("arbitrary",), vmem_limit_bytes=32 * 2**20
        ),
        cost_estimate=pl.CostEstimate(
            flops=16 * slots * own * width, bytes_accessed=12 * slots * width, transcendentals=0
        ),
    )(arrived, arrived, wi, wi_b, wo, wo_b)
    back = send(results)

    keep, give, sums = run(
        combine_kernel, order, (q, gates, stats, back, back, first_full, second_full),
        [whole((tokens, topk))]
        + [whole((tokens, 128))] * 2
        + [rows_block(0), rows_block(1), token_block, token_block],
        (parts_shape, parts_shape, jax.ShapeDtypeStruct((tokens, 128), BF16)),
        (step_block, step_block, whole((tokens, 128))),
        [pltpu.VMEM((tokens, slots), BF16)] * 3
        + [pltpu.VMEM((tokens, slots), F32), pltpu.VMEM((tokens, 128), F32)],
        4 * pick_flops, 4 * slots * width, 24 * 2**20,
    )
    got, got_sums = swap_cores(give), swap_cores(sums)
    halves = [keep[r].astype(F32) + got[r].astype(F32) for r in range(4)]
    sums = join_thirds(sums) + join_thirds(got_sums)
    thirds = split_thirds(sums)
    sent = [jnp.concatenate([halves[r].astype(BF16), thirds], axis=1) for r in (1, 2, 3)]
    arrived, hidden, grad_pre, *sent = lax.optimization_barrier((arrived, hidden, grad_pre, *sent))
    others = [swap_chips(v, r) for r, v in zip((1, 2, 3), sent)]

    x = arrived[:, :half].reshape(slots, width)
    g = arrived[:, half:].reshape(slots, width)
    rows_rows = (((0,), (0,)), ((), ()))
    out_give = lax.dot_general(hidden[:, own:], g, rows_rows, preferred_element_type=F32).astype(BF16)
    out_got = swap_cores(out_give)
    grad_w_out = lax.dot_general(
        hidden[:, :own], g, rows_rows, preferred_element_type=F32
    ) + out_got.astype(F32)
    in_give = lax.dot_general(x, grad_pre[:, own:], rows_rows, preferred_element_type=F32).astype(BF16)
    in_got = swap_cores(in_give)
    grad_w_in = lax.dot_general(
        x, grad_pre[:, :own], rows_rows, preferred_element_type=F32
    ) + in_got.astype(F32)

    *others, grad_w_in, grad_w_out = lax.optimization_barrier((*others, grad_w_in, grad_w_out))
    s1, s2, s3 = [join_thirds(o[:, 2 * part :]) for o in others]
    sums = (sums + s1) + (s2 + s3)
    total = halves[0]
    for o in others:
        total = total + o[:, : 2 * part].astype(F32)
    branch, grad_normed = total[:, :part], total[:, part:]
    stream_input = (stream_second.astype(F32) - branch).astype(BF16)
    mean, rstd = stats[:, 0:1], stats[:, 1:2]
    normed = (stream_first.astype(F32) - mean) * rstd
    correction = grad_normed - sums[:, 4:5] / width - normed * (sums[:, 5:6] / width)
    grad_stream = (grad_first.astype(F32) + rstd * correction).astype(BF16)
    return stream_input, grad_stream, grad_w_in[None], grad_w_out[None], sums[:, :topk]


def solution(mesh):
    wide = Mesh(
        mesh.devices.reshape(4, 2, 4, 4, 2), ("y", "zl", "x", "zh", "core")
    )
    tp = ("zh", "core")
    in_specs = (
        P(CTX, tp),
        P(CTX, tp),
        P(CTX, tp),
        P(CTX, tp),
        P(CTX, None),
        P(CTX, None),
        P(CTX, None, tp),
        P(CTX, tp, None),
    )
    out_specs = (
        P(CTX, tp),
        P(CTX, tp),
        P(CTX, None, tp),
        P(CTX, tp, None),
        P(CTX, None),
    )
    return jax.shard_map(
        on_device, mesh=wide, in_specs=in_specs, out_specs=out_specs, check_vma=False
    )
```

```python
import functools

import jax
import jax.numpy as jnp
from jax import lax
from jax.experimental import pallas as pl
from jax.experimental.pallas import tpu as pltpu
from jax.sharding import Mesh, PartitionSpec as P

F32 = jnp.float32
BF16 = jnp.bfloat16
CTX = ("y", "zl", "x")
CORES = ((0, 1), (1, 0))


def gelu_value(x):
    return x * 0.5 * (1.0 + lax.erf(x * 0.7071067811865476))


def gelu_slope(x):
    return (
        0.5 * (1.0 + lax.erf(x * 0.7071067811865476))
        + x * jnp.exp(-0.5 * x * x) * 0.3989422804014327
    )


def swap_cores(v):
    return lax.ppermute(v, "core", CORES)


def swap_chips(v, r):
    return lax.ppermute(v, "zh", [(i, i ^ r) for i in range(4)])


def gather_chips(v):
    return [v] + [swap_chips(v, r) for r in (1, 2, 3)]


def gather_features(v):
    mine = gather_chips(v)
    return mine + [swap_cores(m) for m in mine]


def select_rows(qt, slots):
    topk, tokens = qt.shape
    at = lax.broadcasted_iota(jnp.int32, (slots, tokens), 0)
    hit = at == qt[0:1, :]
    for k in range(1, topk):
        hit = jnp.logical_or(hit, at == qt[k : k + 1, :])
    return hit


def columns_of(core, mine, other):
    first = core == 0
    left = jnp.where(first, mine, other)
    right = jnp.where(first, other, mine)
    return jnp.concatenate([left, right], axis=1)


def pack_kernel(order, qt_ref, gt_ref, *refs):
    parts, (out_ref, first_ref, second_ref, stats_ref, low, pick, gate) = refs[:8], refs[8:]
    step = pl.program_id(0)
    core = order[4]
    slots = pick.shape[0]
    half = out_ref.shape[1] // 2

    @pl.when(step == 0)
    def _():
        width = 8 * parts[0].shape[2]
        total = sum(jnp.sum(p[0].astype(F32), axis=1, keepdims=True) for p in parts)
        mean = total / width
        square = sum(
            jnp.sum(jnp.square(p[0].astype(F32) - mean), axis=1, keepdims=True) for p in parts
        )
        rstd = lax.rsqrt(square / width + 1e-05)
        for i in range(4):
            both = columns_of(core, parts[i][0].astype(F32), parts[4 + i][0].astype(F32))
            low[i] = ((both - mean) * rstd).astype(BF16)
        lane = lax.broadcasted_iota(jnp.int32, stats_ref.shape, 1)
        stats_ref[...] = jnp.where(lane == 0, mean, rstd)
        qt, gt = qt_ref[...], gt_ref[...]
        pick[...] = jnp.where(select_rows(qt, slots), 1.0, 0.0).astype(BF16)
        at = lax.broadcasted_iota(jnp.int32, (slots, qt.shape[1]), 0)
        weight = jnp.zeros((slots, qt.shape[1]), F32)
        for k in range(qt.shape[0]):
            weight = weight + jnp.where(at == qt[k : k + 1, :], gt[k : k + 1, :], 0.0)
        gate[...] = jnp.sum(weight, axis=1, keepdims=True)

    rows = jnp.dot(pick[...], low[step], preferred_element_type=F32).astype(BF16)
    out_ref[:, :half, :] = rows.reshape(-1, half, rows.shape[1])

    for i in range(4):

        @pl.when(step == i)
        def _(i=i):
            mine, other = parts[i], parts[4 + i]
            first_ref[...] = columns_of(core, mine[0].astype(F32), other[0].astype(F32)).astype(BF16)
            both = columns_of(core, mine[1].astype(F32), other[1].astype(F32)).astype(BF16)
            second_ref[...] = both
            raw = jnp.dot(pick[...], both, preferred_element_type=F32)
            scaled = (gate[...] * raw).astype(BF16)
            out_ref[:, half:, :] = scaled.reshape(-1, half, scaled.shape[1])


def expert_kernel(x_ref, g_ref, wi_a, wi_b, wo_a, wo_b, out_ref, hidden_ref, pre_ref):
    blocks, half, width = x_ref.shape
    own = wi_a.shape[1]
    wide = width // 4
    x = x_ref[...].reshape(blocks * half, width)
    g = g_ref[...].reshape(blocks * half, width)
    last = (((1,), (1,)), ((), ()))
    hidden, grad_pre = [], []
    for wi, wo in ((wi_a, wo_a), (wi_b, wo_b)):
        preact = jnp.dot(x, wi[...], preferred_element_type=F32)
        hidden.append(gelu_value(preact).astype(BF16))
        grad_hidden = lax.dot_general(g, wo[...], last, preferred_element_type=F32)
        grad_pre.append((grad_hidden * gelu_slope(preact)).astype(BF16))
    hidden_ref[:, :own], hidden_ref[:, own:] = hidden
    pre_ref[:, :own], pre_ref[:, own:] = grad_pre
    for n in range(4):
        at = slice(n * wide, (n + 1) * wide)
        value = jnp.dot(hidden[0], wo_a[:, at], preferred_element_type=F32) + jnp.dot(
            hidden[1], wo_b[:, at], preferred_element_type=F32
        )
        out_ref[:, :half, at] = value.astype(BF16).reshape(blocks, half, wide)
        value = lax.dot_general(
            grad_pre[0], wi_a[at, :], last, preferred_element_type=F32
        ) + lax.dot_general(grad_pre[1], wi_b[at, :], last, preferred_element_type=F32)
        out_ref[:, half:, at] = value.astype(BF16).reshape(blocks, half, wide)


def combine_kernel(order, q_ref, g_ref, stats_ref, out_rows, dx_rows, first_ref, second_ref, keep_ref, give_ref, sums_ref, high, rest, pick, inner, sums):
    step = pl.program_id(0)
    part = keep_ref.shape[2] // 2
    slots = pick.shape[1]
    topk = q_ref.shape[1]
    first = order[4] == 0

    @pl.when(step == 0)
    def _():
        lane = lax.broadcasted_iota(jnp.int32, inner.shape, 1)
        weight = jnp.zeros(inner.shape, F32)
        for k in range(topk):
            weight = weight + jnp.where(lane == q_ref[:, k : k + 1], g_ref[:, k : k + 1], 0.0)
        top = weight.astype(BF16)
        high[...] = top
        rest[...] = (weight - top.astype(F32)).astype(BF16)
        hit = lane == q_ref[:, 0:1]
        for k in range(1, topk):
            hit = jnp.logical_or(hit, lane == q_ref[:, k : k + 1])
        pick[...] = jnp.where(hit, 1.0, 0.0).astype(BF16)
        inner[...] = jnp.zeros_like(inner)
        sums[...] = jnp.zeros_like(sums)

    def store(value, at):
        left, right = value[:, :part], value[:, part:]
        keep_ref[0, :, at : at + part] = jnp.where(first, left, right).astype(BF16)
        give_ref[0, :, at : at + part] = jnp.where(first, right, left).astype(BF16)

    rows = out_rows[...].reshape(slots, 2 * part)
    value = jnp.dot(high[...], rows, preferred_element_type=F32) + jnp.dot(
        rest[...], rows, preferred_element_type=F32
    )
    store(value, 0)
    inner[...] += lax.dot_general(
        second_ref[...], rows, (((1,), (1,)), ((), ())), preferred_element_type=F32
    )
    value = jnp.dot(pick[...], dx_rows[...].reshape(slots, 2 * part), preferred_element_type=F32)
    store(value, part)
    normed = (first_ref[...].astype(F32) - stats_ref[:, 0:1]) * stats_ref[:, 1:2]
    lane = lax.broadcasted_iota(jnp.int32, sums.shape, 1)
    place = lane % 8
    plain = jnp.sum(value, axis=1, keepdims=True)
    mixed = jnp.sum(value * normed, axis=1, keepdims=True)
    sums[...] += jnp.where(place == 4, plain, 0.0) + jnp.where(place == 5, mixed, 0.0)

    @pl.when(step == 3)
    def _():
        slot = lax.broadcasted_iota(jnp.int32, inner.shape, 1)
        all_sums = sums[...]
        for k in range(topk):
            one = jnp.sum(
                jnp.where(slot == q_ref[:, k : k + 1], inner[...], 0.0), axis=1, keepdims=True
            )
            all_sums = all_sums + jnp.where(place == k, one, 0.0)
        top = all_sums.astype(BF16).astype(F32)
        middle = (all_sums - top).astype(BF16).astype(F32)
        lowest = all_sums - top - middle
        sums_ref[...] = jnp.where(lane < 8, top, jnp.where(lane < 16, middle, lowest)).astype(BF16)


def join_thirds(v):
    v = v.astype(F32)
    return (v[:, 0:8] + v[:, 8:16]) + v[:, 16:24]


def split_thirds(v):
    high = lax.reduce_precision(v, 8, 7)
    middle = lax.reduce_precision(v - high, 8, 7)
    lowest = v - high - middle
    return jnp.pad(jnp.concatenate([high, middle, lowest], axis=1).astype(BF16), ((0, 0), (0, 104)))


def whole(shape):
    return pl.BlockSpec(shape, lambda i, order: (0,) * len(shape))


def run(kernel, order, args, in_specs, out_shape, out_specs, scratch, flops, moved, limit=None):
    return pl.pallas_call(
        kernel,
        grid_spec=pltpu.PrefetchScalarGridSpec(
            num_scalar_prefetch=1,
            grid=(4,),
            in_specs=in_specs,
            out_specs=out_specs,
            scratch_shapes=scratch,
        ),
        out_shape=out_shape,
        compiler_params=pltpu.CompilerParams(
            dimension_semantics=("arbitrary",), vmem_limit_bytes=limit
        ),
        cost_estimate=pl.CostEstimate(flops=flops, bytes_accessed=moved, transcendentals=0),
    )(order, *args)


def on_device(
    stream_first, stream_second, grad_first, grad_second, expert_ids, gate_probs, w_in, w_out
):
    tokens, part = stream_first.shape
    topk = expert_ids.shape[1]
    width = part * 8
    experts = 32
    half = 16
    slots = experts * half
    core = lax.axis_index("core")
    zh = lax.axis_index("zh")

    expert = jnp.arange(experts, dtype=jnp.int32)
    match = expert_ids[:, :, None] == expert[None, None, :]
    named = jnp.any(match, axis=1).astype(BF16)
    earlier = jnp.tri(tokens, k=-1, dtype=BF16)
    before = jnp.dot(earlier, named, preferred_element_type=F32)
    rank = jnp.sum(jnp.where(match, before[:, None, :], 0.0), axis=2).astype(jnp.int32)
    q = jnp.where(rank % 2 == core, expert_ids * half + rank // 2, -1)
    qt = q.T
    gt = gate_probs.T
    order = jnp.append(jnp.bitwise_xor(zh, jnp.arange(4, dtype=jnp.int32)), core).astype(jnp.int32)

    streams = gather_features(jnp.stack([stream_first, grad_second]))

    token_block = pl.BlockSpec((tokens, 2 * part), lambda i, order: (0, order[i]))
    step_block = pl.BlockSpec((1, tokens, 2 * part), lambda i, order: (i, 0, 0))
    rows_shape = jax.ShapeDtypeStruct((experts, 2 * half, width), BF16)
    full_shape = jax.ShapeDtypeStruct((tokens, width), BF16)
    lane_shape = jax.ShapeDtypeStruct((tokens, 128), F32)
    parts_shape = jax.ShapeDtypeStruct((4, tokens, 2 * part), BF16)
    pick_flops = 2 * slots * tokens * width

    def rows_block(n):
        return pl.BlockSpec((experts, half, 2 * part), lambda i, order: (0, n, order[i]))

    rows, first_full, second_full, stats = run(
        pack_kernel, order, (qt, gt, *streams),
        [whole((topk, tokens))] * 2 + [whole((2, tokens, part))] * 8,
        (rows_shape, full_shape, full_shape, lane_shape),
        (
            pl.BlockSpec((experts, 2 * half, 2 * part), lambda i, order: (0, 0, order[i])),
            token_block, token_block, whole((tokens, 128)),
        ),
        [
            pltpu.VMEM((4, tokens, 2 * part), BF16),
            pltpu.VMEM((slots, tokens), BF16),
            pltpu.VMEM((slots, 1), F32),
        ],
        2 * pick_flops, 4 * slots * width, 24 * 2**20,
    )
    send = functools.partial(
        lax.all_to_all, axis_name=CTX, split_axis=0, concat_axis=0, tiled=True
    )
    wi, wo = w_in[0], w_out[0]
    gates = jnp.pad(gate_probs, ((0, 0), (0, 128 - topk)))
    rows, gates, wi_b, wo_b = lax.optimization_barrier(
        (rows, gates, swap_cores(wi), swap_cores(wo))
    )
    arrived = send(rows)

    own = wo.shape[0]
    step_rows = experts

    def source_block(n):
        return pl.BlockSpec(
            (step_rows, half, width), lambda i: (i, n, 0), pipeline_mode=pl.Buffered(1)
        )

    def fixed(shape):
        return pl.BlockSpec(shape, lambda i: (0, 0), pipeline_mode=pl.Buffered(1))

    unit_block = pl.BlockSpec((step_rows * half, 2 * own), lambda i: (i, 0))
    unit_shape = jax.ShapeDtypeStruct((slots, 2 * own), BF16)
    results, hidden, grad_pre = pl.pallas_call(
        expert_kernel,
        grid=(1,),
        in_specs=[
            source_block(0), source_block(1),
            fixed((width, own)), fixed((width, own)), fixed((own, width)), fixed((own, width)),
        ],
        out_specs=(
            pl.BlockSpec((step_rows, 2 * half, width), lambda i: (i, 0, 0)), unit_block, unit_block
        ),
        out_shape=(rows_shape, unit_shape, unit_shape),
        compiler_params=pltpu.CompilerParams(
            dimension_semantics=("arbitrary",), vmem_limit_bytes=32 * 2**20
        ),
        cost_estimate=pl.CostEstimate(
            flops=16 * slots * own * width, bytes_accessed=12 * slots * width, transcendentals=0
        ),
    )(arrived, arrived, wi, wi_b, wo, wo_b)
    back = send(results)

    keep, give, sums = run(
        combine_kernel, order, (q, gates, stats, back, back, first_full, second_full),
        [whole((tokens, topk))]
        + [whole((tokens, 128))] * 2
        + [rows_block(0), rows_block(1), token_block, token_block],
        (parts_shape, parts_shape, jax.ShapeDtypeStruct((tokens, 128), BF16)),
        (step_block, step_block, whole((tokens, 128))),
        [pltpu.VMEM((tokens, slots), BF16)] * 3
        + [pltpu.VMEM((tokens, slots), F32), pltpu.VMEM((tokens, 128), F32)],
        4 * pick_flops, 4 * slots * width, 24 * 2**20,
    )
    got, got_sums = swap_cores(give), swap_cores(sums)
    halves = [keep[r].astype(F32) + got[r].astype(F32) for r in range(4)]
    sums = join_thirds(sums) + join_thirds(got_sums)
    thirds = split_thirds(sums)
    sent = [jnp.concatenate([halves[r].astype(BF16), thirds], axis=1) for r in (1, 2, 3)]
    arrived, hidden, grad_pre, *sent = lax.optimization_barrier((arrived, hidden, grad_pre, *sent))
    others = [swap_chips(v, r) for r, v in zip((1, 2, 3), sent)]

    x = arrived[:, :half].reshape(slots, width)
    g = arrived[:, half:].reshape(slots, width)
    rows_rows = (((0,), (0,)), ((), ()))
    out_give = lax.dot_general(hidden[:, own:], g, rows_rows, preferred_element_type=F32).astype(BF16)
    out_got = swap_cores(out_give)
    grad_w_out = lax.dot_general(
        hidden[:, :own], g, rows_rows, preferred_element_type=F32
    ) + out_got.astype(F32)
    in_give = lax.dot_general(x, grad_pre[:, own:], rows_rows, preferred_element_type=F32).astype(BF16)
    in_got = swap_cores(in_give)
    grad_w_in = lax.dot_general(
        x, grad_pre[:, :own], rows_rows, preferred_element_type=F32
    ) + in_got.astype(F32)

    *others, grad_w_in, grad_w_out = lax.optimization_barrier((*others, grad_w_in, grad_w_out))
    s1, s2, s3 = [join_thirds(o[:, 2 * part :]) for o in others]
    sums = (sums + s1) + (s2 + s3)
    total = halves[0]
    for o in others:
        total = total + o[:, : 2 * part].astype(F32)
    branch, grad_normed = total[:, :part], total[:, part:]
    stream_input = (stream_second.astype(F32) - branch).astype(BF16)
    mean, rstd = stats[:, 0:1], stats[:, 1:2]
    normed = (stream_first.astype(F32) - mean) * rstd
    correction = grad_normed - sums[:, 4:5] / width - normed * (sums[:, 5:6] / width)
    grad_stream = (grad_first.astype(F32) + rstd * correction).astype(BF16)
    return stream_input, grad_stream, grad_w_in[None], grad_w_out[None], sums[:, :topk]


def solution(mesh):
    wide = Mesh(
        mesh.devices.reshape(4, 2, 4, 4, 2), ("y", "zl", "x", "zh", "core")
    )
    tp = ("zh", "core")
    in_specs = (
        P(CTX, tp),
        P(CTX, tp),
        P(CTX, tp),
        P(CTX, tp),
        P(CTX, None),
        P(CTX, None),
        P(CTX, None, tp),
        P(CTX, tp, None),
    )
    out_specs = (
        P(CTX, tp),
        P(CTX, tp),
        P(CTX, None, tp),
        P(CTX, tp, None),
        P(CTX, None),
    )
    return jax.shard_map(
        on_device, mesh=wide, in_specs=in_specs, out_specs=out_specs, check_vma=False
    )
```
